768 devices in a mesh: fsdp: 96 (over y_lo, z, x), group: 8 (over y_hi, core).
Axes of the slice: x: 4, y: 8 (y_hi: 4, y_lo: 2; y = y_hi * 2 + y_lo), z: 12, core: 2. Of those that a mesh axis runs over, the one named last changes fastest.
Arguments:
- query_rows: bfloat16 [96, 8, 128, 3072], P('fsdp', 'group'), may hold values from -40 to 40
- key_rows: bfloat16 [96, 8, 128, 3072], P('fsdp', 'group'), may hold values from -40 to 40
- value_rows: bfloat16 [96, 8, 128, 3072], P('fsdp', 'group'), may hold values from -6 to 6
- out_grad: bfloat16 [96, 8, 152, 3072], P('fsdp', 'group'), may hold values from -12 to 12
- query_gain: float32 [3072], P('fsdp'), may hold values from 0.5 to 1.5
- key_gain: float32 [3072], P('fsdp'), may hold values from 0.5 to 1.5
- image_sizes: int32 [96, 8, 4], P('fsdp', 'group'), may hold values from 16 to 72, as said below
- sends_tail: int32 [96, 8], P('fsdp', 'group'), may hold values from 0 to 1, as said below
Outputs:
- d_query: bfloat16 [96, 8, 128, 3072], P('fsdp', 'group')
- d_key: bfloat16 [96, 8, 128, 3072], P('fsdp', 'group')
- d_query_gain: float32 [3072], P('fsdp')
- d_key_gain: float32 [3072], P('fsdp')
The draws below stay inside these ranges and needn't reach their ends.
Inputs may be any that keep to these rules, and one draw needn't show every extreme that they name: `image_sizes`: the last image of every shard has exactly 24 patches, the others 16 or more; each shard's images together fill its 128 rows. `sends_tail`: of a shard and its partner exactly one holds 1: the one whose images' squared patch counts sum larger, on equal sums the one of lower group index.
All inputs are finite; a program needn't handle non-finite values.
Results may differ from the reference program's by a relative error of at most 0.0069.
Values may be sent and summed in bfloat16 or wider, within the bound.
A program may use at most 32 MiB of HBM per device.

```python
import jax
import jax.numpy as jnp
from jax import lax

HEADS = 24
DH = 128
WID = 3072
ROWS = 128
SEND = 24
MINP = 16
IMGS = 4
DROWS = 152
N_FSDP = 96
N_GROUP = 8


def draw_query_rows(key, part):
    key = jax.random.fold_in(key, 3)
    entry_key, scale_key = jax.random.split(key)
    row_scale = jnp.exp(jax.random.uniform(scale_key, (N_FSDP, N_GROUP, ROWS, HEADS, 1), jnp.float32, 0.0, 2.3))
    entries = jnp.clip(jax.random.normal(entry_key, (N_FSDP, N_GROUP, ROWS, HEADS, DH), jnp.float32), -4.0, 4.0)
    return (entries * row_scale).reshape(N_FSDP, N_GROUP, ROWS, HEADS * DH).astype(jnp.bfloat16)


def draw_key_rows(key, part):
    key = jax.random.fold_in(key, 4)
    entry_key, scale_key = jax.random.split(key)
    row_scale = jnp.exp(jax.random.uniform(scale_key, (N_FSDP, N_GROUP, ROWS, HEADS, 1), jnp.float32, 0.0, 2.3))
    entries = jnp.clip(jax.random.normal(entry_key, (N_FSDP, N_GROUP, ROWS, HEADS, DH), jnp.float32), -4.0, 4.0)
    return (entries * row_scale).reshape(N_FSDP, N_GROUP, ROWS, HEADS * DH).astype(jnp.bfloat16)


def image_layout(key):
    key = jax.random.fold_in(key, 7)
    first_key, second_key, pick_key = jax.random.split(key, 3)
    head_total = ROWS - SEND
    grid_shape = (N_FSDP, N_GROUP)
    largest = head_total - 2 * MINP
    first_size = jax.random.randint(first_key, grid_shape, MINP, largest + 1)
    chosen = jax.random.randint(pick_key, (), 0, N_FSDP * N_GROUP)
    marked = (jnp.arange(N_FSDP * N_GROUP, dtype=jnp.int32) == chosen).reshape(grid_shape)
    first_size = jnp.where(marked, largest, first_size).astype(jnp.int32)
    second_size = jax.random.randint(second_key, grid_shape, MINP, head_total - first_size - MINP + 1)
    third_size = head_total - first_size - second_size
    last_size = jnp.full(grid_shape, SEND, jnp.int32)
    return jnp.stack([first_size, second_size, third_size, last_size], axis=-1).astype(jnp.int32)


def draw_image_sizes(key, part):
    return image_layout(key)


def draw_sends_tail(key, part):
    sizes = image_layout(key)
    load = jnp.sum(sizes * sizes, axis=-1).astype(jnp.int32)
    group_index = jnp.arange(N_GROUP, dtype=jnp.int32)
    partner = jnp.bitwise_xor(group_index, N_GROUP // 2)
    other_load = load[:, partner]
    heavier = (load > other_load) | (load == other_load) & (group_index[None, :] < partner[None, :])
    return heavier.astype(jnp.int32)


def block_scale(rng, extent, cuts, low, top_value):
    gain = 1.0
    for dim, shards_of in cuts:
        heights = jax.random.uniform(jax.random.fold_in(jax.random.fold_in(rng, 6), dim), (shards_of,), jnp.float32, low / len(cuts), top_value / len(cuts))
        gain = gain * jnp.repeat(jnp.exp(heights), extent[dim] // shards_of).reshape((-1,) + (1,) * (len(extent) - 1 - dim))
    return gain


def bell_draw(stream_key, shape, scale, most, cuts=(), kind=jnp.bfloat16):
    factor_of = block_scale(stream_key, shape, cuts, -0.22, 0.18) if cuts else 1.0
    values = jax.random.normal(stream_key, shape, jnp.float32) * scale * factor_of
    return jnp.minimum(jnp.maximum(values, -most), most).astype(kind)


def setup_inputs(seed: int = 0) -> dict:
    streams_of = jax.random.split(jax.random.key(seed), 9)
    query_rows = draw_query_rows(jax.random.fold_in(streams_of[8], 71), 0)
    key_rows = draw_key_rows(jax.random.fold_in(streams_of[8], 71), 0)
    value_rows = bell_draw(streams_of[2], (N_FSDP, N_GROUP, ROWS, WID), 1.0, 6.0, ((0, 96), (1, 8)))
    out_grad = bell_draw(streams_of[3], (N_FSDP, N_GROUP, DROWS, WID), 2.0, 12.0, ((0, 96), (1, 8)))
    query_gain = jnp.clip(0.5 + 1.0 * jax.random.uniform(streams_of[4], (WID,), jnp.float32) ** block_scale(streams_of[4], (WID,), ((0, 96),), -0.2, 0.2), 0.5, 1.5)
    key_gain = jnp.clip(0.5 + 1.0 * jax.random.uniform(streams_of[5], (WID,), jnp.float32) ** block_scale(streams_of[5], (WID,), ((0, 96),), -0.2, 0.2), 0.5, 1.5)
    image_sizes = draw_image_sizes(jax.random.fold_in(streams_of[8], 71), 0)
    sends_tail = draw_sends_tail(jax.random.fold_in(streams_of[8], 71), 0)
    return {"query_rows": query_rows, "key_rows": key_rows, "value_rows": value_rows, "out_grad": out_grad, "query_gain": query_gain, "key_gain": key_gain, "image_sizes": image_sizes, "sends_tail": sends_tail}


EPSILON = 1e-06

def normalize(values):
    center = values - lax.optimization_barrier(jnp.mean(values, axis=-1, keepdims=True))
    inverse = lax.rsqrt(lax.optimization_barrier(jnp.mean(center * center, axis=-1, keepdims=True)) + EPSILON)
    return (center * inverse, inverse)

def norm_backward(grad_hat, row_hat, inverse):
    mean_grad = lax.optimization_barrier(jnp.mean(grad_hat, axis=-1, keepdims=True))
    mean_cross = lax.optimization_barrier(jnp.mean(grad_hat * row_hat, axis=-1, keepdims=True))
    return (grad_hat - mean_grad - row_hat * mean_cross) * inverse

def attend(buf_query, buf_key, buf_value, buf_grad, gain_query, gain_key, row_ids):
    row_count = buf_query.shape[0]
    head_count = buf_query.shape[1] // DH
    score_scale = DH ** (-0.5)
    query_hat, query_inv = normalize(buf_query.reshape(row_count, head_count, DH).astype(jnp.float32))
    key_hat, key_inv = normalize(buf_key.reshape(row_count, head_count, DH).astype(jnp.float32))
    gain_q = gain_query.reshape(head_count, DH)
    gain_k = gain_key.reshape(head_count, DH)
    query_norm = (query_hat * gain_q).astype(jnp.bfloat16)
    key_norm = (key_hat * gain_k).astype(jnp.bfloat16)
    scores = jnp.einsum('qhd,khd->hqk', query_norm.astype(jnp.float32), key_norm.astype(jnp.float32)) * score_scale
    same_image = ((row_ids[:, None] == row_ids[None, :]) & (row_ids[:, None] >= 0)).astype(jnp.float32)
    live_rows = (row_ids >= 0).astype(jnp.float32)
    weights = jnp.exp(scores) * same_image[None, :, :]
    attention = weights / (lax.optimization_barrier(jnp.sum(weights, axis=-1)) + (1.0 - live_rows)[None, :])[:, :, None]
    value_rows = buf_value.reshape(row_count, head_count, DH).astype(jnp.float32)
    grad_rows = buf_grad.reshape(row_count, head_count, DH).astype(jnp.float32)
    grad_probs = jnp.einsum('qhd,khd->hqk', grad_rows, value_rows)
    carried = lax.optimization_barrier(jnp.sum(attention * grad_probs, axis=-1))
    grad_scores = (attention * (grad_probs - carried[:, :, None]) * score_scale).astype(jnp.bfloat16)
    grad_qn = jnp.einsum('hqk,khd->qhd', grad_scores.astype(jnp.float32), key_norm.astype(jnp.float32))
    grad_kn = jnp.einsum('hqk,qhd->khd', grad_scores.astype(jnp.float32), query_norm.astype(jnp.float32))
    grad_query = norm_backward(grad_qn * gain_q, query_hat, query_inv)
    grad_key = norm_backward(grad_kn * gain_k, key_hat, key_inv)
    term_query = lax.optimization_barrier(jnp.sum(grad_qn * query_hat, axis=0)).reshape(-1)
    term_key = lax.optimization_barrier(jnp.sum(grad_kn * key_hat, axis=0)).reshape(-1)
    return (grad_query.reshape(row_count, -1).astype(jnp.bfloat16), grad_key.reshape(row_count, -1).astype(jnp.bfloat16), term_query, term_key)

def reference(query_rows, key_rows, value_rows, out_grad, query_gain, key_gain, image_sizes, sends_tail):
    shards = N_FSDP * N_GROUP
    partner = jnp.bitwise_xor(jnp.arange(N_GROUP, dtype=jnp.int32), N_GROUP // 2)
    head_rows = ROWS - SEND

    def tail_of(array):
        return array[:, partner, head_rows:].reshape(shards, SEND, WID)

    def one_shard(pieces):
        own_q, own_k, own_v, tail_q, tail_k, tail_v, grad_rows, size_list, is_sender = pieces
        image_ends = jnp.cumsum(size_list).astype(jnp.int32)
        places = jnp.arange(ROWS, dtype=jnp.int32)
        own_ids = lax.optimization_barrier(jnp.sum((places[:, None] >= image_ends[None, :]).astype(jnp.int32), axis=1)).astype(jnp.int32)
        own_ids = jnp.where((is_sender == 1) & (own_ids == IMGS - 1), -1, own_ids).astype(jnp.int32)
        extra_ids = (jnp.full((SEND,), IMGS, jnp.int32) * (1 - is_sender) - is_sender).astype(jnp.int32)
        row_ids = jnp.concatenate([own_ids, extra_ids]).astype(jnp.int32)
        return attend(jnp.concatenate([own_q, tail_q]), jnp.concatenate([own_k, tail_k]), jnp.concatenate([own_v, tail_v]), grad_rows, query_gain, key_gain, row_ids)
    results = lax.map(one_shard, (query_rows.reshape(shards, ROWS, WID), key_rows.reshape(shards, ROWS, WID), value_rows.reshape(shards, ROWS, WID), tail_of(query_rows), tail_of(key_rows), tail_of(value_rows), out_grad.reshape(shards, DROWS, WID), image_sizes.reshape(shards, IMGS), sends_tail.reshape(shards)))
    query_buffers, key_buffers, terms_query, terms_key = results

    def place(buffers):
        buffers = buffers.reshape(N_FSDP, N_GROUP, DROWS, WID)
        moved_back = buffers[:, partner, ROWS:]
        tail_block = jnp.where(sends_tail[:, :, None, None] == 1, moved_back, buffers[:, :, head_rows:ROWS])
        return jnp.concatenate([buffers[:, :, :head_rows], tail_block], axis=2)
    return (place(query_buffers), place(key_buffers), lax.optimization_barrier(jnp.sum(terms_query, axis=0)), lax.optimization_barrier(jnp.sum(terms_key, axis=0)))
```

```python
import functools
import math

import jax
import jax.numpy as jnp
from jax import lax
from jax.experimental import pallas as pl
from jax.experimental.pallas import tpu as pltpu
from jax.sharding import PartitionSpec as P

DH = 128
EPSILON = 1e-06
SCALE = DH ** (-0.5)
EXP_SCALE = SCALE * math.log2(math.e)
MESH = pl.DeviceIdType.MESH


def normalize(values):
    center = values - jnp.sum(values, axis=-1, keepdims=True) * (1.0 / DH)
    variance = jnp.sum(center * center, axis=-1, keepdims=True) * (1.0 / DH)
    inverse = lax.rsqrt(variance + EPSILON)
    return center * inverse, inverse


def norm_backward(grad_normed, row_hat, inverse, gain):
    cross = grad_normed * row_hat
    grad_hat = grad_normed * gain
    mean_grad = jnp.sum(grad_hat, axis=-1, keepdims=True) * (1.0 / DH)
    mean_cross = jnp.sum(cross * gain, axis=-1, keepdims=True) * (1.0 / DH)
    grad = (grad_hat - mean_grad - row_hat * mean_cross) * inverse
    return grad.astype(jnp.bfloat16), jnp.sum(cross, axis=0, keepdims=True)


def dot(left, right, left_dim, right_dim):
    return lax.dot_general(
        left, right, (((left_dim,), (right_dim,)), ((), ())), preferred_element_type=jnp.float32
    )


def kernel(
    sizes,
    q_hbm,
    k_hbm,
    v_hbm,
    g_hbm,
    gain_q_ref,
    gain_k_ref,
    sizes_ref,
    sends_ref,
    dq_hbm,
    dk_hbm,
    gains_out,
    q_buf,
    k_buf,
    v_buf,
    g_buf,
    q_hat,
    k_hat,
    q_inv,
    k_inv,
    dq_buf,
    dk_buf,
    same,
    tail_out,
    tail_in,
    parts,
    gains,
    terms,
    first,
    last,
    load_sem,
    store_sem,
    parts_sem,
    gains_sem,
    tail_send,
    tail_recv,
    first_sem,
    last_sem,
):
    heads, quarters, groups, rows, tail = sizes
    pairs = heads // 2
    crew = quarters * groups
    keep = rows - tail
    f = lax.axis_index("fsdp")
    g = lax.axis_index("group")
    head = f // quarters
    quarter = f % quarters
    mine = quarter * groups + g
    partner = (f, (g + groups // 2) % groups)

    def head_peer(step):
        other = (head + step) % heads
        return other, (other * quarters + quarter, g)

    def crew_peer(step):
        other = (mine + step) % crew
        return other, (head * quarters + other // groups, other % groups)

    def quarter_peer(step):
        other = (quarter + step) % quarters
        return other, (head * quarters + other, g)

    barrier = pltpu.get_barrier_semaphore()

    def greet_head(step, carry):
        pl.semaphore_signal(barrier, inc=1, device_id=head_peer(step)[1], device_id_type=MESH)
        return carry

    def greet_crew(step, carry):
        pl.semaphore_signal(barrier, inc=1, device_id=crew_peer(step)[1], device_id_type=MESH)
        return carry

    lax.fori_loop(1, heads, greet_head, 0)
    lax.fori_loop(1, crew, greet_crew, 0)

    loads = [
        pltpu.make_async_copy(src, dst, load_sem.at[i])
        for i, (src, dst) in enumerate(
            ((g_hbm, g_buf), (q_hbm, q_buf), (k_hbm, k_buf), (v_hbm, v_buf))
        )
    ]
    for load in loads:
        load.start()

    lane_quarter = lax.broadcasted_iota(jnp.int32, (1, DH), 1) // (DH // quarters)
    own_gains = jnp.concatenate(
        [
            jnp.concatenate([gain_ref[...]] * quarters, axis=1)
            for gain_ref in (gain_q_ref, gain_k_ref)
        ],
        axis=0,
    )
    parts[quarter] = jnp.where(lane_quarter == quarter, own_gains, 0.0)

    row_ids = jnp.zeros((rows, rows), jnp.int32)
    col_ids = jnp.zeros((rows, rows), jnp.int32)
    row_place = lax.broadcasted_iota(jnp.int32, (rows, rows), 0)
    col_place = lax.broadcasted_iota(jnp.int32, (rows, rows), 1)
    end = jnp.int32(0)
    for i in range(sizes_ref.shape[1]):
        end = end + sizes_ref[0, i]
        row_ids += (row_place >= end).astype(jnp.int32)
        col_ids += (col_place >= end).astype(jnp.int32)
    same[...] = (row_ids == col_ids).astype(jnp.float32)

    loads[0].wait()

    def pack_tail(pair, carry):
        lanes = pl.ds(pl.multiple_of(pair * 2 * DH, 2 * DH), 2 * DH)
        block = g_buf[rows : rows + tail, lanes].astype(jnp.float32)
        stacked = jnp.concatenate([block[:, :DH], block[:, DH:]], axis=0)
        tail_out[pair] = stacked.astype(jnp.bfloat16)
        return carry

    lax.fori_loop(0, pairs, pack_tail, 0)

    pl.semaphore_wait(barrier, heads - 1 + crew - 1)

    def send_part(step, carry):
        pltpu.make_async_remote_copy(
            src_ref=parts.at[quarter],
            dst_ref=parts.at[quarter],
            send_sem=parts_sem.at[0],
            recv_sem=parts_sem.at[1],
            device_id=quarter_peer(step)[1],
            device_id_type=MESH,
        ).start()
        return carry

    lax.fori_loop(1, quarters, send_part, 0)

    def pair_at(step):
        return (head // 2 + 1 + step) % pairs

    def tail_copy(step):
        pair = pair_at(step)
        return pltpu.make_async_remote_copy(
            src_ref=tail_out.at[pair],
            dst_ref=tail_in.at[pair],
            send_sem=tail_send.at[step],
            recv_sem=tail_recv.at[step],
            device_id=partner,
            device_id_type=MESH,
        )

    def send_tail(step, carry):
        tail_copy(step).start()
        return carry

    def wait_all(buffer, count, sem):
        span = buffer.at[pl.ds(0, count)]
        pltpu.make_async_copy(span, span, sem).wait()

    wait_all(parts, quarters - 1, parts_sem.at[0])
    wait_all(parts, quarters - 1, parts_sem.at[1])
    gains[head] = jnp.sum(parts[...], axis=0)

    def send_gain(step, carry):
        pltpu.make_async_remote_copy(
            src_ref=gains.at[head],
            dst_ref=gains.at[head],
            send_sem=gains_sem.at[0],
            recv_sem=gains_sem.at[1],
            device_id=head_peer(step)[1],
            device_id_type=MESH,
        ).start()
        return carry

    lax.fori_loop(1, heads, send_gain, 0)
    lax.fori_loop(0, pairs, send_tail, 0)

    loads[1].wait()
    loads[2].wait()

    def normalize_pair(pair, carry):
        for half in range(2):
            lanes = pl.ds(pl.multiple_of((pair * 2 + half) * DH, DH), DH)
            for src, hat, inv in ((q_buf, q_hat, q_inv), (k_buf, k_hat, k_inv)):
                row_hat, inverse = normalize(src[:, lanes].astype(jnp.float32))
                hat[:, lanes] = row_hat
                inv[:, lanes] = jnp.broadcast_to(inverse, row_hat.shape)
        return carry

    lax.fori_loop(0, pairs, normalize_pair, 0)
    loads[3].wait()
    wait_all(gains, heads - 1, gains_sem.at[0])
    wait_all(gains, heads - 1, gains_sem.at[1])

    sender = jnp.broadcast_to(sends_ref[0, 0], (tail, DH)) == 1
    low = keep // 16 * 16
    fixed = keep - low

    def attend(index, moved):
        lanes = pl.ds(pl.multiple_of(index * DH, DH), DH)
        gain_q = gains[index, 0:1, :]
        gain_k = gains[index, 1:2, :]
        edge = g_buf[low:rows, lanes].astype(jnp.float32)
        edge = jnp.concatenate([edge[:fixed], jnp.where(sender, moved, edge[fixed:])], axis=0)
        grads = jnp.concatenate([g_buf[:low, lanes], edge.astype(jnp.bfloat16)], axis=0)
        query_hat = q_hat[:, lanes]
        key_hat = k_hat[:, lanes]
        query_norm = (query_hat * gain_q).astype(jnp.bfloat16)
        key_norm = (key_hat * gain_k).astype(jnp.bfloat16)
        scores = dot(query_norm, key_norm, 1, 1)
        weights = jnp.exp2(scores * EXP_SCALE) * same[...]
        grad_probs = dot(grads, v_buf[:, lanes], 1, 1)
        scale = 1.0 / jnp.sum(weights, axis=-1, keepdims=True)
        carried = jnp.sum(weights * grad_probs, axis=-1, keepdims=True) * scale
        grad_scores = (weights * (scale * SCALE) * (grad_probs - carried)).astype(jnp.bfloat16)
        grad_qn = dot(grad_scores, key_norm, 1, 0)
        grad_kn = dot(grad_scores, query_norm, 0, 0)
        grad_q, term_q = norm_backward(grad_qn, query_hat, q_inv[:, lanes], gain_q)
        grad_k, term_k = norm_backward(grad_kn, key_hat, k_inv[:, lanes], gain_k)
        dq_buf[:, lanes] = grad_q
        dk_buf[:, lanes] = grad_k
        terms[index, 0:1, :] = term_q
        terms[index, 1:2, :] = term_k

    def attend_pair(step, carry):
        pair = pair_at(step)
        tail_copy(step).wait()
        moved = tail_in[pair].astype(jnp.float32)
        for half in range(2):
            attend(pair * 2 + half, moved[half * tail : (half + 1) * tail])
        lanes = pl.ds(pl.multiple_of(pair * 2 * DH, 2 * DH), 2 * DH)
        pltpu.make_async_copy(dq_buf.at[:, lanes], dq_hbm.at[:, lanes], store_sem.at[0]).start()
        pltpu.make_async_copy(dk_buf.at[:, lanes], dk_hbm.at[:, lanes], store_sem.at[1]).start()
        for half in range(2):
            index = pair * 2 + half

            @pl.when(index != head)
            def _():
                pltpu.make_async_remote_copy(
                    src_ref=terms.at[index],
                    dst_ref=first.at[head],
                    send_sem=first_sem.at[0],
                    recv_sem=first_sem.at[1],
                    device_id=(index * quarters + quarter, g),
                    device_id_type=MESH,
                ).start()

        return carry

    lax.fori_loop(0, pairs, attend_pair, 0)

    first[head] = terms[head]
    wait_all(first, heads - 1, first_sem.at[1])
    last[mine] = jnp.sum(first[...], axis=0)

    def send_last(step, carry):
        pltpu.make_async_remote_copy(
            src_ref=last.at[mine],
            dst_ref=last.at[mine],
            send_sem=last_sem.at[0],
            recv_sem=last_sem.at[1],
            device_id=crew_peer(step)[1],
            device_id_type=MESH,
        ).start()
        return carry

    lax.fori_loop(1, crew, send_last, 0)
    wait_all(first, heads - 1, first_sem.at[0])
    pltpu.make_async_copy(dq_buf, dq_hbm, store_sem.at[0]).wait()
    pltpu.make_async_copy(dk_buf, dk_hbm, store_sem.at[1]).wait()
    wait_all(last, crew - 1, last_sem.at[0])
    wait_all(last, crew - 1, last_sem.at[1])
    total = jnp.sum(last[...], axis=0)
    width = DH // quarters
    piece = jnp.zeros((2, width), jnp.float32)
    for i in range(quarters):
        piece += jnp.where(quarter == i, total[:, i * width : (i + 1) * width], 0.0)
    gains_out[...] = piece


def body(query_rows, key_rows, value_rows, out_grad, query_gain, key_gain, image_sizes, sends_tail):
    _, _, rows, wid = query_rows.shape
    grad_rows = out_grad.shape[2]
    tail = grad_rows - rows
    heads = wid // DH
    quarters = lax.axis_size("fsdp") // heads
    groups = lax.axis_size("group")
    pairs = heads // 2
    crew = quarters * groups
    width = DH // quarters
    any_spec = pl.BlockSpec(memory_space=pltpu.HBM)
    vmem = pl.BlockSpec(memory_space=pltpu.VMEM)
    smem = pl.BlockSpec(memory_space=pltpu.SMEM)
    wide = (rows, wid)
    dma = pltpu.SemaphoreType.DMA
    dq, dk, gains = pl.pallas_call(
        functools.partial(kernel, (heads, quarters, groups, rows, tail)),
        out_shape=(
            jax.ShapeDtypeStruct(wide, jnp.bfloat16),
            jax.ShapeDtypeStruct(wide, jnp.bfloat16),
            jax.ShapeDtypeStruct((2, width), jnp.float32),
        ),
        in_specs=[any_spec] * 4 + [vmem] * 2 + [smem] * 2,
        out_specs=(any_spec, any_spec, vmem),
        scratch_shapes=[
            pltpu.VMEM(wide, jnp.bfloat16),
            pltpu.VMEM(wide, jnp.bfloat16),
            pltpu.VMEM(wide, jnp.bfloat16),
            pltpu.VMEM((grad_rows, wid), jnp.bfloat16),
            pltpu.VMEM(wide, jnp.float32),
            pltpu.VMEM(wide, jnp.float32),
            pltpu.VMEM(wide, jnp.float32),
            pltpu.VMEM(wide, jnp.float32),
            pltpu.VMEM(wide, jnp.bfloat16),
            pltpu.VMEM(wide, jnp.bfloat16),
            pltpu.VMEM((rows, rows), jnp.float32),
            pltpu.VMEM((pairs, 2 * tail, DH), jnp.bfloat16),
            pltpu.VMEM((pairs, 2 * tail, DH), jnp.bfloat16),
            pltpu.VMEM((quarters, 2, DH), jnp.float32),
            pltpu.VMEM((heads, 2, DH), jnp.float32),
            pltpu.VMEM((heads, 2, DH), jnp.float32),
            pltpu.VMEM((heads, 2, DH), jnp.float32),
            pltpu.VMEM((crew, 2, DH), jnp.float32),
            dma((4,)),
            dma((2,)),
            dma((2,)),
            dma((2,)),
            dma((pairs,)),
            dma((pairs,)),
            dma((2,)),
            dma((2,)),
        ],
        compiler_params=pltpu.CompilerParams(
            collective_id=0, has_side_effects=True, vmem_limit_bytes=48 * 1024 * 1024
        ),
    )(
        query_rows.reshape(wide),
        key_rows.reshape(wide),
        value_rows.reshape(wide),
        out_grad.reshape(grad_rows, wid),
        query_gain.reshape(1, width),
        key_gain.reshape(1, width),
        image_sizes.reshape(1, -1),
        sends_tail,
    )
    return dq[None, None], dk[None, None], gains[0], gains[1]


def solution(mesh):
    placed = (
        P("fsdp", "group", None, None),
        P("fsdp", "group", None, None),
        P("fsdp", "group", None, None),
        P("fsdp", "group", None, None),
        P("fsdp"),
        P("fsdp"),
        P("fsdp", "group", None),
        P("fsdp", "group"),
    )
    return jax.shard_map(
        body,
        mesh=mesh,
        in_specs=placed,
        out_specs=(
            P("fsdp", "group", None, None),
            P("fsdp", "group", None, None),
            P("fsdp"),
            P("fsdp"),
        ),
        check_vma=False,
    )
```

```python
import functools
import math

import jax
import jax.numpy as jnp
from jax import lax
from jax.experimental import pallas as pl
from jax.experimental.pallas import tpu as pltpu
from jax.sharding import PartitionSpec as P

DH = 128
EPSILON = 1e-06
SCALE = DH ** (-0.5)
EXP_SCALE = SCALE * math.log2(math.e)
MESH = pl.DeviceIdType.MESH
CHUNKS = 4
VMEM_LIMIT = 48 * 1024 * 1024


def normalize(values):
    center = values - jnp.sum(values, axis=-1, keepdims=True) * (1.0 / DH)
    variance = jnp.sum(center * center, axis=-1, keepdims=True) * (1.0 / DH)
    inverse = lax.rsqrt(variance + EPSILON)
    return center * inverse, inverse


def norm_backward(grad_normed, row_hat, inverse, gain):
    cross = grad_normed * row_hat
    grad_hat = grad_normed * gain
    mean_grad = jnp.sum(grad_hat, axis=-1, keepdims=True) * (1.0 / DH)
    mean_cross = jnp.sum(cross * gain, axis=-1, keepdims=True) * (1.0 / DH)
    grad = (grad_hat - mean_grad - row_hat * mean_cross) * inverse
    return grad.astype(jnp.bfloat16), jnp.sum(cross, axis=0, keepdims=True)


def dot(left, right, right_dim):
    return lax.dot_general(
        left, right, (((1,), (right_dim,)), ((), ())), preferred_element_type=jnp.float32
    )


def diagonal(first, second):
    zero = jnp.zeros_like(first)
    return jnp.concatenate(
        [jnp.concatenate([first, zero], axis=1), jnp.concatenate([zero, second], axis=1)], axis=0
    )


def side_by_side(pieces):
    return jnp.concatenate(pieces, axis=1)


def kernel(
    sizes,
    q_hbm,
    k_hbm,
    v_hbm,
    g_hbm,
    gain_q_hbm,
    gain_k_hbm,
    sizes_hbm,
    sends_ref,
    dq_out,
    dk_out,
    gains_out,
    q_buf,
    k_buf,
    v_buf,
    g_buf,
    gain_buf,
    sizes_buf,
    q_hat,
    k_hat,
    q_inv,
    k_inv,
    dq_buf,
    dk_buf,
    same,
    tail_out,
    tail_in,
    parts,
    gains,
    terms,
    first,
    last,
    load_sem,
    store_sem,
    parts_sem,
    gains_send,
    gains_recv,
    tail_send,
    tail_recv,
    first_sem,
    last_sem,
):
    heads, quarters, groups, rows, tail = sizes
    pairs = heads // 2
    width = DH // quarters
    crew = quarters * groups
    keep = rows - tail
    f = lax.axis_index("fsdp")
    g = lax.axis_index("group")
    head = f // quarters
    quarter = f % quarters
    mine = quarter * groups + g
    partner = (f, (g + groups // 2) % groups)

    def by_line(action, lines):
        def visit(step, carry):
            for other in (lines(step), lines(step) + pairs):
                pl.when(other != head)(functools.partial(action, (other * quarters + quarter, g)))
            return carry

        lax.fori_loop(0, pairs, visit, 0)

    def crew_peer(step):
        other = (mine + step) % crew
        return (head * quarters + other // groups, other % groups)

    def quarter_peer(step):
        return (head * quarters + (quarter + step) % quarters, g)

    barrier = pltpu.get_barrier_semaphore()

    def greet(peer):
        def signal(step, carry):
            pl.semaphore_signal(barrier, inc=1, device_id=peer(step), device_id_type=MESH)
            return carry

        return signal

    by_line(
        lambda peer: pl.semaphore_signal(barrier, inc=1, device_id=peer, device_id_type=MESH),
        lambda step: step,
    )
    lax.fori_loop(1, crew, greet(crew_peer), 0)

    loads = [
        pltpu.make_async_copy(src, dst, load_sem.at[i])
        for i, (src, dst) in enumerate(
            (
                (gain_q_hbm, gain_buf.at[0]),
                (gain_k_hbm, gain_buf.at[1]),
                (sizes_hbm, sizes_buf),
                (g_hbm, g_buf),
                (q_hbm, q_buf),
                (k_hbm, k_buf),
                (v_hbm, v_buf),
            )
        )
    ]
    for load in loads:
        load.start()
    for load in loads[:3]:
        load.wait()

    lane_quarter = lax.broadcasted_iota(jnp.int32, (1, DH), 1) // width
    own_gains = jnp.concatenate([side_by_side([gain_buf[i]] * quarters) for i in range(2)], axis=0)
    parts[quarter] = jnp.where(lane_quarter == quarter, own_gains, 0.0)

    row_ids = jnp.zeros((rows, rows), jnp.int32)
    col_ids = jnp.zeros((rows, rows), jnp.int32)
    row_place = lax.broadcasted_iota(jnp.int32, (rows, rows), 0)
    col_place = lax.broadcasted_iota(jnp.int32, (rows, rows), 1)
    end = jnp.int32(0)
    for i in range(sizes_buf.shape[1]):
        end = end + sizes_buf[0, i]
        row_ids += (row_place >= end).astype(jnp.int32)
        col_ids += (col_place >= end).astype(jnp.int32)
    same[...] = (row_ids == col_ids).astype(jnp.float32)

    def lanes_of(index):
        return pl.ds(pl.multiple_of(index * DH, DH), DH)

    loads[3].wait()

    def pack_tail(pair, carry):
        stacked = jnp.concatenate(
            [g_buf[rows : rows + tail, lanes_of(pair + i * pairs)] for i in range(2)], axis=1
        ).astype(jnp.float32)
        stacked = jnp.concatenate([stacked[:, :DH], stacked[:, DH:]], axis=0)
        tail_out[pair] = stacked.astype(jnp.bfloat16)
        return carry

    lax.fori_loop(0, pairs, pack_tail, 0)

    def normalize_all(src, hat, inv):
        def normalize_pair(pair, carry):
            for i in range(2):
                lanes = lanes_of(pair * 2 + i)
                row_hat, inverse = normalize(src[:, lanes].astype(jnp.float32))
                hat[:, lanes] = row_hat
                inv[:, lanes] = jnp.broadcast_to(inverse, row_hat.shape)
            return carry

        lax.fori_loop(0, pairs, normalize_pair, 0)

    loads[4].wait()
    normalize_all(q_buf, q_hat, q_inv)

    pl.semaphore_wait(barrier, heads - 1 + crew - 1)

    def send_part(step, carry):
        pltpu.make_async_remote_copy(
            src_ref=parts.at[quarter],
            dst_ref=parts.at[quarter],
            send_sem=parts_sem.at[0],
            recv_sem=parts_sem.at[1],
            device_id=quarter_peer(step),
            device_id_type=MESH,
        ).start()
        return carry

    lax.fori_loop(1, quarters, send_part, 0)

    def pair_at(step):
        return step

    def tail_copy(step):
        pair = pair_at(step)
        return pltpu.make_async_remote_copy(
            src_ref=tail_out.at[pair],
            dst_ref=tail_in.at[pair],
            send_sem=tail_send.at[step],
            recv_sem=tail_recv.at[step],
            device_id=partner,
            device_id_type=MESH,
        )

    def send_tail(step, carry):
        tail_copy(step).start()
        return carry

    lax.fori_loop(0, pairs, send_tail, 0)

    def wait_all(buffer, count, sem):
        span = buffer.at[pl.ds(0, count)]
        pltpu.make_async_copy(span, span, sem).wait()

    loads[5].wait()
    normalize_all(k_buf, k_hat, k_inv)

    wait_all(parts, quarters - 1, parts_sem.at[1])
    gains[head] = jnp.sum(parts[...], axis=0)

    def send_gain(peer):
        pltpu.make_async_remote_copy(
            src_ref=gains.at[head],
            dst_ref=gains.at[head],
            send_sem=gains_send.at[0],
            recv_sem=gains_recv.at[head],
            device_id=peer,
            device_id_type=MESH,
        ).start()

    by_line(send_gain, lambda step: pairs - 1 - step)

    loads[6].wait()
    sender = jnp.broadcast_to(sends_ref[0, 0], (tail, 2 * DH)) == 1
    low = keep // 16 * 16
    fixed = keep - low

    def attend(pair):
        indices = (pair, pair + pairs)
        lanes = [lanes_of(i) for i in indices]
        gain_q = [gains[i, 0:1, :] for i in indices]
        gain_k = [gains[i, 1:2, :] for i in indices]
        moved = tail_in[pair].astype(jnp.float32)
        moved = side_by_side([moved[:tail], moved[tail:]])
        edge = side_by_side([g_buf[low:rows, at] for at in lanes]).astype(jnp.float32)
        edge = jnp.concatenate([edge[:fixed], jnp.where(sender, moved, edge[fixed:])], axis=0)
        grads = side_by_side([g_buf[:low, at] for at in lanes])
        grads = jnp.concatenate([grads, edge.astype(jnp.bfloat16)], axis=0)
        query_hat = [q_hat[:, at] for at in lanes]
        key_hat = [k_hat[:, at] for at in lanes]
        query_norm = [(hat * gain).astype(jnp.bfloat16) for hat, gain in zip(query_hat, gain_q)]
        key_norm = [(hat * gain).astype(jnp.bfloat16) for hat, gain in zip(key_hat, gain_k)]
        keys = diagonal(*key_norm)
        scores = dot(side_by_side(query_norm), keys, 1)
        grad_probs = dot(grads, diagonal(*[v_buf[:, at] for at in lanes]), 1)
        grad_scores = []
        for i in range(2):
            half = slice(i * rows, (i + 1) * rows)
            weights = jnp.exp2(scores[:, half] * EXP_SCALE) * same[...]
            probs = grad_probs[:, half]
            scale = 1.0 / jnp.sum(weights, axis=-1, keepdims=True)
            carried = jnp.sum(weights * probs, axis=-1, keepdims=True) * scale
            grad_scores.append((weights * (scale * SCALE) * (probs - carried)).astype(jnp.bfloat16))
        grad_qn = dot(side_by_side(grad_scores), keys, 0)
        grad_kn = dot(side_by_side([x.T for x in grad_scores]), diagonal(*query_norm), 0)
        for i, index in enumerate(indices):
            half = slice(i * DH, (i + 1) * DH)
            at = lanes[i]
            grad_q, term_q = norm_backward(grad_qn[:, half], query_hat[i], q_inv[:, at], gain_q[i])
            grad_k, term_k = norm_backward(grad_kn[:, half], key_hat[i], k_inv[:, at], gain_k[i])
            dq_buf[:, at] = grad_q
            dk_buf[:, at] = grad_k
            terms[index, 0:1, :] = term_q
            terms[index, 1:2, :] = term_k

    batch = 2 if pairs % 2 == 0 else 1

    def attend_batch(turn, carry):
        todo = [pair_at(turn * batch + i) for i in range(batch)]
        for i, pair in enumerate(todo):
            for index in (pair, pair + pairs):

                @pl.when(index != head)
                def _():
                    row = gains.at[index]
                    pltpu.make_async_copy(row, row, gains_recv.at[index]).wait()

            tail_copy(turn * batch + i).wait()
        for pair in todo:
            attend(pair)
        for pair in todo:
            for index in (pair, pair + pairs):

                @pl.when(index != head)
                def _():
                    pltpu.make_async_remote_copy(
                        src_ref=terms.at[index],
                        dst_ref=first.at[head],
                        send_sem=first_sem.at[0],
                        recv_sem=first_sem.at[1],
                        device_id=(index * quarters + quarter, g),
                        device_id_type=MESH,
                    ).start()

        for pair in todo:
            for index in (pair, pair + pairs):
                at = lanes_of(index)
                pltpu.make_async_copy(dq_buf.at[:, at], dq_out.at[:, at], store_sem.at[0]).start()
                pltpu.make_async_copy(dk_buf.at[:, at], dk_out.at[:, at], store_sem.at[1]).start()
        return carry

    lax.fori_loop(0, pairs // batch, attend_batch, 0)

    first[head] = terms[head]
    wait_all(first, heads - 1, first_sem.at[1])
    last[mine] = jnp.sum(first[...], axis=0)

    def send_last(step, carry):
        pltpu.make_async_remote_copy(
            src_ref=last.at[mine],
            dst_ref=last.at[mine],
            send_sem=last_sem.at[0],
            recv_sem=last_sem.at[1],
            device_id=crew_peer(step),
            device_id_type=MESH,
        ).start()
        return carry

    lax.fori_loop(1, crew, send_last, 0)
    wait_all(parts, quarters - 1, parts_sem.at[0])
    wait_all(gains, heads - 1, gains_send.at[0])
    wait_all(first, heads - 1, first_sem.at[0])
    pltpu.make_async_copy(dq_buf, dq_out, store_sem.at[0]).wait()
    pltpu.make_async_copy(dk_buf, dk_out, store_sem.at[1]).wait()
    wait_all(last, crew - 1, last_sem.at[0])
    wait_all(last, crew - 1, last_sem.at[1])
    total = jnp.sum(last[...], axis=0)
    piece = jnp.zeros((2, width), jnp.float32)
    for i in range(quarters):
        piece += jnp.where(quarter == i, total[:, i * width : (i + 1) * width], 0.0)
    gains_out[...] = piece


def finish(dq_in, dk_in, gains_in, dq_out, dk_out, gain_q_out, gain_k_out, sem):
    rows = dq_in.shape[0]
    chunk = rows // CHUNKS
    copies = [
        pltpu.make_async_copy(
            src.at[pl.ds(i * chunk, chunk)], dst.at[pl.ds(i * chunk, chunk)], sem.at[j * CHUNKS + i]
        )
        for i in range(CHUNKS)
        for j, (src, dst) in enumerate(((dq_in, dq_out), (dk_in, dk_out)))
    ]
    for copy in copies:
        copy.start()
    gain_q_out[...] = gains_in[0:1, :]
    gain_k_out[...] = gains_in[1:2, :]
    for copy in copies:
        copy.wait()


def body(query_rows, key_rows, value_rows, out_grad, query_gain, key_gain, image_sizes, sends_tail):
    _, _, rows, wid = query_rows.shape
    grad_rows = out_grad.shape[2]
    tail = grad_rows - rows
    heads = wid // DH
    quarters = lax.axis_size("fsdp") // heads
    groups = lax.axis_size("group")
    pairs = heads // 2
    crew = quarters * groups
    width = DH // quarters
    any_spec = pl.BlockSpec(memory_space=pl.ANY)
    vmem = pl.BlockSpec(memory_space=pltpu.VMEM)
    wide = (rows, wid)
    dma = pltpu.SemaphoreType.DMA
    images = image_sizes.shape[-1]
    operands = (
        query_rows.reshape(wide),
        key_rows.reshape(wide),
        value_rows.reshape(wide),
        out_grad.reshape(grad_rows, wid),
        query_gain.reshape(1, width),
        key_gain.reshape(1, width),
        image_sizes.reshape(1, images),
    )
    dq, dk, gains = pl.pallas_call(
        functools.partial(kernel, (heads, quarters, groups, rows, tail)),
        out_shape=(
            jax.ShapeDtypeStruct(wide, jnp.bfloat16),
            jax.ShapeDtypeStruct(wide, jnp.bfloat16),
            jax.ShapeDtypeStruct((2, width), jnp.float32),
        ),
        in_specs=[any_spec] * 7 + [pl.BlockSpec(memory_space=pltpu.SMEM)],
        out_specs=(any_spec, any_spec, vmem),
        scratch_shapes=[
            pltpu.VMEM(wide, jnp.bfloat16),
            pltpu.VMEM(wide, jnp.bfloat16),
            pltpu.VMEM(wide, jnp.bfloat16),
            pltpu.VMEM((grad_rows, wid), jnp.bfloat16),
            pltpu.VMEM((2, 1, width), jnp.float32),
            pltpu.SMEM((1, images), jnp.int32),
            pltpu.VMEM(wide, jnp.float32),
            pltpu.VMEM(wide, jnp.float32),
            pltpu.VMEM(wide, jnp.float32),
            pltpu.VMEM(wide, jnp.float32),
            pltpu.VMEM(wide, jnp.bfloat16),
            pltpu.VMEM(wide, jnp.bfloat16),
            pltpu.VMEM((rows, rows), jnp.float32),
            pltpu.VMEM((pairs, 2 * tail, DH), jnp.bfloat16),
            pltpu.VMEM((pairs, 2 * tail, DH), jnp.bfloat16),
            pltpu.VMEM((quarters, 2, DH), jnp.float32),
            pltpu.VMEM((heads, 2, DH), jnp.float32),
            pltpu.VMEM((heads, 2, DH), jnp.float32),
            pltpu.VMEM((heads, 2, DH), jnp.float32),
            pltpu.VMEM((crew, 2, DH), jnp.float32),
            dma((7,)),
            dma((2,)),
            dma((2,)),
            dma((1,)),
            dma((heads,)),
            dma((pairs,)),
            dma((pairs,)),
            dma((2,)),
            dma((2,)),
        ],
        compiler_params=pltpu.CompilerParams(
            collective_id=0, has_side_effects=True, vmem_limit_bytes=VMEM_LIMIT
        ),
    )(*[pltpu.with_memory_space_constraint(x, pltpu.HBM) for x in operands], sends_tail)
    dq, dk, gain_q, gain_k = pl.pallas_call(
        finish,
        out_shape=(
            jax.ShapeDtypeStruct(wide, jnp.bfloat16),
            jax.ShapeDtypeStruct(wide, jnp.bfloat16),
            jax.ShapeDtypeStruct((1, width), jnp.float32),
            jax.ShapeDtypeStruct((1, width), jnp.float32),
        ),
        in_specs=[vmem, vmem, vmem],
        out_specs=(any_spec, any_spec, vmem, vmem),
        scratch_shapes=[dma((2 * CHUNKS,))],
    )(*[pltpu.with_memory_space_constraint(x, pltpu.VMEM) for x in (dq, dk, gains)])
    return dq[None, None], dk[None, None], gain_q.reshape(width), gain_k.reshape(width)


def solution(mesh):
    placed = (
        P("fsdp", "group", None, None),
        P("fsdp", "group", None, None),
        P("fsdp", "group", None, None),
        P("fsdp", "group", None, None),
        P("fsdp"),
        P("fsdp"),
        P("fsdp", "group", None),
        P("fsdp", "group"),
    )
    return jax.shard_map(
        body,
        mesh=mesh,
        in_specs=placed,
        out_specs=(
            P("fsdp", "group", None, None),
            P("fsdp", "group", None, None),
            P("fsdp"),
            P("fsdp"),
        ),
        check_vma=False,
    )
```

```python
import functools
import math

import jax
import jax.numpy as jnp
from jax import lax
from jax.experimental import pallas as pl
from jax.experimental.pallas import tpu as pltpu
from jax.sharding import PartitionSpec as P

DH = 128
EPSILON = 1e-06
SCALE = DH ** (-0.5)
EXP_SCALE = SCALE * math.log2(math.e)
MESH = pl.DeviceIdType.MESH
CHUNKS = 4
VMEM_LIMIT = 48 * 1024 * 1024


def normalize(values):
    center = values - jnp.sum(values, axis=-1, keepdims=True) * (1.0 / DH)
    variance = jnp.sum(center * center, axis=-1, keepdims=True) * (1.0 / DH)
    inverse = lax.rsqrt(variance + EPSILON)
    return center * inverse, inverse


def norm_backward(grad_normed, row_hat, inverse, gain):
    cross = grad_normed * row_hat
    grad_hat = grad_normed * gain
    mean_grad = jnp.sum(grad_hat, axis=-1, keepdims=True) * (1.0 / DH)
    mean_cross = jnp.sum(cross * gain, axis=-1, keepdims=True) * (1.0 / DH)
    grad = (grad_hat - mean_grad - row_hat * mean_cross) * inverse
    return grad.astype(jnp.bfloat16), jnp.sum(cross, axis=0, keepdims=True)


def dot(left, right, right_dim):
    return lax.dot_general(
        left, right, (((1,), (right_dim,)), ((), ())), preferred_element_type=jnp.float32
    )


def diagonal(first, second):
    zero = jnp.zeros_like(first)
    return jnp.concatenate(
        [jnp.concatenate([first, zero], axis=1), jnp.concatenate([zero, second], axis=1)], axis=0
    )


def side_by_side(pieces):
    return jnp.concatenate(pieces, axis=1)


def kernel(
    sizes,
    q_hbm,
    k_hbm,
    v_hbm,
    g_hbm,
    gain_q_hbm,
    gain_k_hbm,
    sizes_hbm,
    sends_ref,
    dq_out,
    dk_out,
    gains_out,
    q_buf,
    k_buf,
    v_buf,
    g_buf,
    gain_buf,
    sizes_buf,
    q_hat,
    k_hat,
    q_inv,
    k_inv,
    dq_buf,
    dk_buf,
    same,
    tail_out,
    tail_in,
    parts,
    gains,
    terms,
    first,
    last,
    load_sem,
    store_sem,
    parts_sem,
    gains_send,
    gains_recv,
    tail_send,
    tail_recv,
    first_sem,
    last_sem,
):
    heads, quarters, groups, rows, tail = sizes
    pairs = heads // 2
    width = DH // quarters
    crew = quarters * groups
    keep = rows - tail
    f = lax.axis_index("fsdp")
    g = lax.axis_index("group")
    head = f // quarters
    quarter = f % quarters
    mine = quarter * groups + g
    partner = (f, (g + groups // 2) % groups)

    def by_line(action, lines):
        def visit(step, carry):
            for other in (lines(step), lines(step) + pairs):
                pl.when(other != head)(functools.partial(action, (other * quarters + quarter, g)))
            return carry

        lax.fori_loop(0, pairs, visit, 0)

    def far_first(count):
        return sorted(range(count), key=lambda step: -min(step, count - step))

    crew_peers = [
        (head * quarters + (quarter + across) % quarters, (g + along) % groups)
        for along in far_first(groups)
        for across in far_first(quarters)
    ][:-1]

    def quarter_peer(step):
        return (head * quarters + (quarter + step) % quarters, g)

    barrier = pltpu.get_barrier_semaphore()

    by_line(
        lambda peer: pl.semaphore_signal(barrier, inc=1, device_id=peer, device_id_type=MESH),
        lambda step: step,
    )
    for peer in crew_peers:
        pl.semaphore_signal(barrier, inc=1, device_id=peer, device_id_type=MESH)

    loads = [
        pltpu.make_async_copy(src, dst, load_sem.at[i])
        for i, (src, dst) in enumerate(
            (
                (gain_q_hbm, gain_buf.at[0]),
                (gain_k_hbm, gain_buf.at[1]),
                (sizes_hbm, sizes_buf),
                (g_hbm, g_buf),
                (q_hbm, q_buf),
                (k_hbm, k_buf),
                (v_hbm, v_buf),
            )
        )
    ]
    for load in loads:
        load.start()
    for load in loads[:3]:
        load.wait()

    lane_quarter = lax.broadcasted_iota(jnp.int32, (1, DH), 1) // width
    own_gains = jnp.concatenate([side_by_side([gain_buf[i]] * quarters) for i in range(2)], axis=0)
    parts[quarter] = jnp.where(lane_quarter == quarter, own_gains, 0.0)

    row_ids = jnp.zeros((rows, rows), jnp.int32)
    col_ids = jnp.zeros((rows, rows), jnp.int32)
    row_place = lax.broadcasted_iota(jnp.int32, (rows, rows), 0)
    col_place = lax.broadcasted_iota(jnp.int32, (rows, rows), 1)
    end = jnp.int32(0)
    for i in range(sizes_buf.shape[1]):
        end = end + sizes_buf[0, i]
        row_ids += (row_place >= end).astype(jnp.int32)
        col_ids += (col_place >= end).astype(jnp.int32)
    same[...] = (row_ids == col_ids).astype(jnp.float32)

    def lanes_of(index):
        return pl.ds(pl.multiple_of(index * DH, DH), DH)

    loads[3].wait()

    def pack_tail(pair, carry):
        stacked = jnp.concatenate(
            [g_buf[rows : rows + tail, lanes_of(pair + i * pairs)] for i in range(2)], axis=1
        ).astype(jnp.float32)
        stacked = jnp.concatenate([stacked[:, :DH], stacked[:, DH:]], axis=0)
        tail_out[pair] = stacked.astype(jnp.bfloat16)
        return carry

    lax.fori_loop(0, pairs, pack_tail, 0)

    def normalize_all(src, hat, inv):
        def normalize_pair(pair, carry):
            for i in range(2):
                lanes = lanes_of(pair * 2 + i)
                row_hat, inverse = normalize(src[:, lanes].astype(jnp.float32))
                hat[:, lanes] = row_hat
                inv[:, lanes] = jnp.broadcast_to(inverse, row_hat.shape)
            return carry

        lax.fori_loop(0, pairs, normalize_pair, 0)

    loads[4].wait()
    normalize_all(q_buf, q_hat, q_inv)

    pl.semaphore_wait(barrier, heads - 1 + crew - 1)

    def send_part(step, carry):
        pltpu.make_async_remote_copy(
            src_ref=parts.at[quarter],
            dst_ref=parts.at[quarter],
            send_sem=parts_sem.at[0],
            recv_sem=parts_sem.at[1],
            device_id=quarter_peer(step),
            device_id_type=MESH,
        ).start()
        return carry

    lax.fori_loop(1, quarters, send_part, 0)

    def pair_at(step):
        return step

    def tail_copy(step):
        pair = pair_at(step)
        return pltpu.make_async_remote_copy(
            src_ref=tail_out.at[pair],
            dst_ref=tail_in.at[pair],
            send_sem=tail_send.at[step],
            recv_sem=tail_recv.at[step],
            device_id=partner,
            device_id_type=MESH,
        )

    def send_tail(step, carry):
        tail_copy(step).start()
        return carry

    lax.fori_loop(0, pairs, send_tail, 0)

    def wait_all(buffer, count, sem):
        span = buffer.at[pl.ds(0, count)]
        pltpu.make_async_copy(span, span, sem).wait()

    loads[5].wait()
    normalize_all(k_buf, k_hat, k_inv)

    wait_all(parts, quarters - 1, parts_sem.at[1])
    gains[head] = jnp.sum(parts[...], axis=0)

    def send_gain(peer):
        pltpu.make_async_remote_copy(
            src_ref=gains.at[head],
            dst_ref=gains.at[head],
            send_sem=gains_send.at[0],
            recv_sem=gains_recv.at[head],
            device_id=peer,
            device_id_type=MESH,
        ).start()

    by_line(send_gain, lambda step: pairs - 1 - step)

    loads[6].wait()
    sender = jnp.broadcast_to(sends_ref[0, 0], (tail, 2 * DH)) == 1
    low = keep // 16 * 16
    fixed = keep - low

    def attend(pair):
        indices = (pair, pair + pairs)
        lanes = [lanes_of(i) for i in indices]
        gain_q = [gains[i, 0:1, :] for i in indices]
        gain_k = [gains[i, 1:2, :] for i in indices]
        moved = tail_in[pair].astype(jnp.float32)
        moved = side_by_side([moved[:tail], moved[tail:]])
        edge = side_by_side([g_buf[low:rows, at] for at in lanes]).astype(jnp.float32)
        edge = jnp.concatenate([edge[:fixed], jnp.where(sender, moved, edge[fixed:])], axis=0)
        grads = side_by_side([g_buf[:low, at] for at in lanes])
        grads = jnp.concatenate([grads, edge.astype(jnp.bfloat16)], axis=0)
        query_hat = [q_hat[:, at] for at in lanes]
        key_hat = [k_hat[:, at] for at in lanes]
        query_norm = [(hat * gain).astype(jnp.bfloat16) for hat, gain in zip(query_hat, gain_q)]
        key_norm = [(hat * gain).astype(jnp.bfloat16) for hat, gain in zip(key_hat, gain_k)]
        keys = diagonal(*key_norm)
        scores = dot(side_by_side(query_norm), keys, 1)
        grad_probs = dot(grads, diagonal(*[v_buf[:, at] for at in lanes]), 1)
        grad_scores = []
        for i in range(2):
            half = slice(i * rows, (i + 1) * rows)
            weights = jnp.exp2(scores[:, half] * EXP_SCALE) * same[...]
            probs = grad_probs[:, half]
            scale = 1.0 / jnp.sum(weights, axis=-1, keepdims=True)
            carried = jnp.sum(weights * probs, axis=-1, keepdims=True) * scale
            grad_scores.append((weights * (scale * SCALE) * (probs - carried)).astype(jnp.bfloat16))
        grad_qn = dot(side_by_side(grad_scores), keys, 0)
        grad_kn = dot(side_by_side([x.T for x in grad_scores]), diagonal(*query_norm), 0)
        for i, index in enumerate(indices):
            half = slice(i * DH, (i + 1) * DH)
            at = lanes[i]
            grad_q, term_q = norm_backward(grad_qn[:, half], query_hat[i], q_inv[:, at], gain_q[i])
            grad_k, term_k = norm_backward(grad_kn[:, half], key_hat[i], k_inv[:, at], gain_k[i])
            dq_buf[:, at] = grad_q
            dk_buf[:, at] = grad_k
            terms[index, 0:1, :] = term_q
            terms[index, 1:2, :] = term_k

    batch = 2 if pairs % 2 == 0 else 1

    def attend_batch(turn, carry):
        todo = [pair_at(turn * batch + i) for i in range(batch)]
        for i, pair in enumerate(todo):
            for index in (pair, pair + pairs):

                @pl.when(index != head)
                def _():
                    row = gains.at[index]
                    pltpu.make_async_copy(row, row, gains_recv.at[index]).wait()

            tail_copy(turn * batch + i).wait()
        for pair in todo:
            attend(pair)
        for pair in todo:
            for index in (pair, pair + pairs):

                @pl.when(index != head)
                def _():
                    pltpu.make_async_remote_copy(
                        src_ref=terms.at[index],
                        dst_ref=first.at[head],
                        send_sem=first_sem.at[0],
                        recv_sem=first_sem.at[1],
                        device_id=(index * quarters + quarter, g),
                        device_id_type=MESH,
                    ).start()

        for pair in todo:
            for index in (pair, pair + pairs):
                at = lanes_of(index)
                pltpu.make_async_copy(dq_buf.at[:, at], dq_out.at[:, at], store_sem.at[0]).start()
                pltpu.make_async_copy(dk_buf.at[:, at], dk_out.at[:, at], store_sem.at[1]).start()
        return carry

    lax.fori_loop(0, pairs // batch, attend_batch, 0)

    first[head] = terms[head]
    wait_all(first, heads - 1, first_sem.at[1])
    last[mine] = jnp.sum(first[...], axis=0)

    for peer in crew_peers:
        pltpu.make_async_remote_copy(
            src_ref=last.at[mine],
            dst_ref=last.at[mine],
            send_sem=last_sem.at[0],
            recv_sem=last_sem.at[1],
            device_id=peer,
            device_id_type=MESH,
        ).start()
    wait_all(parts, quarters - 1, parts_sem.at[0])
    wait_all(gains, heads - 1, gains_send.at[0])
    wait_all(first, heads - 1, first_sem.at[0])
    pltpu.make_async_copy(dq_buf, dq_out, store_sem.at[0]).wait()
    pltpu.make_async_copy(dk_buf, dk_out, store_sem.at[1]).wait()
    wait_all(last, crew - 1, last_sem.at[0])
    wait_all(last, crew - 1, last_sem.at[1])
    total = jnp.sum(last[...], axis=0)
    piece = jnp.zeros((2, width), jnp.float32)
    for i in range(quarters):
        piece += jnp.where(quarter == i, total[:, i * width : (i + 1) * width], 0.0)
    for i in range(2):
        gains_out[i] = piece[i : i + 1]


def finish(dq_in, dk_in, gains_in, dq_out, dk_out, gain_q_out, gain_k_out, sem):
    rows = dq_in.shape[0]
    chunk = rows // CHUNKS
    copies = [
        pltpu.make_async_copy(
            src.at[pl.ds(i * chunk, chunk)], dst.at[pl.ds(i * chunk, chunk)], sem.at[j * CHUNKS + i]
        )
        for i in range(CHUNKS)
        for j, (src, dst) in enumerate(((dq_in, dq_out), (dk_in, dk_out)))
    ]
    copies += [
        pltpu.make_async_copy(gains_in.at[i], out, sem.at[2 * CHUNKS + i])
        for i, out in enumerate((gain_q_out, gain_k_out))
    ]
    for copy in copies:
        copy.start()
    for copy in copies:
        copy.wait()


def body(query_rows, key_rows, value_rows, out_grad, query_gain, key_gain, image_sizes, sends_tail):
    _, _, rows, wid = query_rows.shape
    grad_rows = out_grad.shape[2]
    tail = grad_rows - rows
    heads = wid // DH
    quarters = lax.axis_size("fsdp") // heads
    groups = lax.axis_size("group")
    pairs = heads // 2
    crew = quarters * groups
    width = DH // quarters
    any_spec = pl.BlockSpec(memory_space=pl.ANY)
    vmem = pl.BlockSpec(memory_space=pltpu.VMEM)
    wide = (rows, wid)
    dma = pltpu.SemaphoreType.DMA
    images = image_sizes.shape[-1]
    operands = (
        query_rows.reshape(wide),
        key_rows.reshape(wide),
        value_rows.reshape(wide),
        out_grad.reshape(grad_rows, wid),
        query_gain.reshape(1, width),
        key_gain.reshape(1, width),
        image_sizes.reshape(1, images),
    )
    dq, dk, gains = pl.pallas_call(
        functools.partial(kernel, (heads, quarters, groups, rows, tail)),
        out_shape=(
            jax.ShapeDtypeStruct(wide, jnp.bfloat16),
            jax.ShapeDtypeStruct(wide, jnp.bfloat16),
            jax.ShapeDtypeStruct((2, 1, width), jnp.float32),
        ),
        in_specs=[any_spec] * 7 + [pl.BlockSpec(memory_space=pltpu.SMEM)],
        out_specs=(any_spec, any_spec, vmem),
        scratch_shapes=[
            pltpu.VMEM(wide, jnp.bfloat16),
            pltpu.VMEM(wide, jnp.bfloat16),
            pltpu.VMEM(wide, jnp.bfloat16),
            pltpu.VMEM((grad_rows, wid), jnp.bfloat16),
            pltpu.VMEM((2, 1, width), jnp.float32),
            pltpu.SMEM((1, images), jnp.int32),
            pltpu.VMEM(wide, jnp.float32),
            pltpu.VMEM(wide, jnp.float32),
            pltpu.VMEM(wide, jnp.float32),
            pltpu.VMEM(wide, jnp.float32),
            pltpu.VMEM(wide, jnp.bfloat16),
            pltpu.VMEM(wide, jnp.bfloat16),
            pltpu.VMEM((rows, rows), jnp.float32),
            pltpu.VMEM((pairs, 2 * tail, DH), jnp.bfloat16),
            pltpu.VMEM((pairs, 2 * tail, DH), jnp.bfloat16),
            pltpu.VMEM((quarters, 2, DH), jnp.float32),
            pltpu.VMEM((heads, 2, DH), jnp.float32),
            pltpu.VMEM((heads, 2, DH), jnp.float32),
            pltpu.VMEM((heads, 2, DH), jnp.float32),
            pltpu.VMEM((crew, 2, DH), jnp.float32),
            dma((7,)),
            dma((2,)),
            dma((2,)),
            dma((1,)),
            dma((heads,)),
            dma((pairs,)),
            dma((pairs,)),
            dma((2,)),
            dma((2,)),
        ],
        compiler_params=pltpu.CompilerParams(
            collective_id=0, has_side_effects=True, vmem_limit_bytes=VMEM_LIMIT
        ),
    )(*[pltpu.with_memory_space_constraint(x, pltpu.HBM) for x in operands], sends_tail)
    dq, dk, gain_q, gain_k = pl.pallas_call(
        finish,
        out_shape=(
            jax.ShapeDtypeStruct(wide, jnp.bfloat16),
            jax.ShapeDtypeStruct(wide, jnp.bfloat16),
            jax.ShapeDtypeStruct((1, width), jnp.float32),
            jax.ShapeDtypeStruct((1, width), jnp.float32),
        ),
        in_specs=[vmem, vmem, vmem],
        out_specs=(any_spec,) * 4,
        scratch_shapes=[dma((2 * CHUNKS + 2,))],
    )(*[pltpu.with_memory_space_constraint(x, pltpu.VMEM) for x in (dq, dk, gains)])
    return dq[None, None], dk[None, None], gain_q.reshape(width), gain_k.reshape(width)


def solution(mesh):
    placed = (
        P("fsdp", "group", None, None),
        P("fsdp", "group", None, None),
        P("fsdp", "group", None, None),
        P("fsdp", "group", None, None),
        P("fsdp"),
        P("fsdp"),
        P("fsdp", "group", None),
        P("fsdp", "group"),
    )
    return jax.shard_map(
        body,
        mesh=mesh,
        in_specs=placed,
        out_specs=(
            P("fsdp", "group", None, None),
            P("fsdp", "group", None, None),
            P("fsdp"),
            P("fsdp"),
        ),
        check_vma=False,
    )
```

```python
import functools
import math

import jax
import jax.numpy as jnp
from jax import lax
from jax.experimental import pallas as pl
from jax.experimental.pallas import tpu as pltpu
from jax.sharding import PartitionSpec as P

DH = 128
EPSILON = 1e-06
SCALE = DH ** (-0.5)
EXP_SCALE = SCALE * math.log2(math.e)
MESH = pl.DeviceIdType.MESH
CHUNKS = 4
VMEM_LIMIT = 48 * 1024 * 1024


def normalize(values):
    center = values - jnp.sum(values, axis=-1, keepdims=True) * (1.0 / DH)
    variance = jnp.sum(center * center, axis=-1, keepdims=True) * (1.0 / DH)
    inverse = lax.rsqrt(variance + EPSILON)
    return center * inverse, inverse


def norm_backward(grad_normed, row_hat, inverse, gain):
    cross = grad_normed * row_hat
    grad_hat = grad_normed * gain
    mean_grad = jnp.sum(grad_hat, axis=-1, keepdims=True) * (1.0 / DH)
    mean_cross = jnp.sum(cross * gain, axis=-1, keepdims=True) * (1.0 / DH)
    grad = (grad_hat - mean_grad - row_hat * mean_cross) * inverse
    return grad.astype(jnp.bfloat16), jnp.sum(cross, axis=0, keepdims=True)


def dot(left, right, right_dim):
    return lax.dot_general(
        left, right, (((1,), (right_dim,)), ((), ())), preferred_element_type=jnp.float32
    )


def diagonal(first, second):
    zero = jnp.zeros_like(first)
    return jnp.concatenate(
        [jnp.concatenate([first, zero], axis=1), jnp.concatenate([zero, second], axis=1)], axis=0
    )


def side_by_side(pieces):
    return jnp.concatenate(pieces, axis=1)


def kernel(
    sizes,
    q_hbm,
    k_hbm,
    v_hbm,
    g_hbm,
    gain_q_hbm,
    gain_k_hbm,
    sizes_hbm,
    sends_ref,
    dq_out,
    dk_out,
    gains_out,
    q_buf,
    k_buf,
    v_buf,
    g_buf,
    gain_buf,
    sizes_buf,
    q_hat,
    k_hat,
    q_inv,
    k_inv,
    dq_buf,
    dk_buf,
    same,
    tail_out,
    tail_in,
    parts,
    gains,
    terms,
    first,
    last,
    load_sem,
    store_sem,
    parts_sem,
    gains_send,
    gains_recv,
    tail_send,
    tail_recv,
    first_sem,
    last_sem,
):
    heads, quarters, groups, rows, tail = sizes
    pairs = heads // 2
    width = DH // quarters
    crew = quarters * groups
    keep = rows - tail
    f = lax.axis_index("fsdp")
    g = lax.axis_index("group")
    head = f // quarters
    quarter = f % quarters
    mine = quarter * groups + g
    partner = (f, (g + groups // 2) % groups)

    def by_line(action, lines):
        def visit(step, carry):
            for other in (lines(step), lines(step) + pairs):
                pl.when(other != head)(functools.partial(action, (other * quarters + quarter, g)))
            return carry

        lax.fori_loop(0, pairs, visit, 0)

    def far_first(count):
        return sorted(range(count), key=lambda step: -min(step, count - step))

    crew_peers = [
        (head * quarters + (quarter + across) % quarters, (g + along) % groups)
        for along in far_first(groups)
        for across in far_first(quarters)
    ][:-1]

    def quarter_peer(step):
        return (head * quarters + (quarter + step) % quarters, g)

    barrier = pltpu.get_barrier_semaphore()

    by_line(
        lambda peer: pl.semaphore_signal(barrier, inc=1, device_id=peer, device_id_type=MESH),
        lambda step: step,
    )
    for peer in crew_peers:
        pl.semaphore_signal(barrier, inc=1, device_id=peer, device_id_type=MESH)

    loads = [
        pltpu.make_async_copy(src, dst, load_sem.at[i])
        for i, (src, dst) in enumerate(
            (
                (gain_q_hbm, gain_buf.at[0]),
                (gain_k_hbm, gain_buf.at[1]),
                (sizes_hbm, sizes_buf),
                (g_hbm, g_buf),
                (q_hbm, q_buf),
                (k_hbm, k_buf),
                (v_hbm, v_buf),
            )
        )
    ]
    for load in loads:
        load.start()
    for load in loads[:3]:
        load.wait()

    lane_quarter = lax.broadcasted_iota(jnp.int32, (1, DH), 1) // width
    own_gains = jnp.concatenate([side_by_side([gain_buf[i]] * quarters) for i in range(2)], axis=0)
    parts[quarter] = jnp.where(lane_quarter == quarter, own_gains, 0.0)

    row_ids = jnp.zeros((rows, rows), jnp.int32)
    col_ids = jnp.zeros((rows, rows), jnp.int32)
    row_place = lax.broadcasted_iota(jnp.int32, (rows, rows), 0)
    col_place = lax.broadcasted_iota(jnp.int32, (rows, rows), 1)
    end = jnp.int32(0)
    for i in range(sizes_buf.shape[1]):
        end = end + sizes_buf[0, i]
        row_ids += (row_place >= end).astype(jnp.int32)
        col_ids += (col_place >= end).astype(jnp.int32)
    same[...] = (row_ids == col_ids).astype(jnp.float32)

    def lanes_of(index):
        return pl.ds(pl.multiple_of(index * DH, DH), DH)

    loads[3].wait()

    def pack_tail(pair, carry):
        stacked = jnp.concatenate(
            [g_buf[rows : rows + tail, lanes_of(pair + i * pairs)] for i in range(2)], axis=1
        ).astype(jnp.float32)
        stacked = jnp.concatenate([stacked[:, :DH], stacked[:, DH:]], axis=0)
        tail_out[pair] = stacked.astype(jnp.bfloat16)
        return carry

    lax.fori_loop(0, pairs, pack_tail, 0)

    def normalize_all(src, hat, inv):
        def normalize_pair(pair, carry):
            for i in range(2):
                lanes = lanes_of(pair * 2 + i)
                row_hat, inverse = normalize(src[:, lanes].astype(jnp.float32))
                hat[:, lanes] = row_hat
                inv[:, lanes] = jnp.broadcast_to(inverse, row_hat.shape)
            return carry

        lax.fori_loop(0, pairs, normalize_pair, 0)

    loads[4].wait()
    normalize_all(q_buf, q_hat, q_inv)

    pl.semaphore_wait(barrier, heads - 1 + crew - 1)

    def send_part(step, carry):
        pltpu.make_async_remote_copy(
            src_ref=parts.at[quarter],
            dst_ref=parts.at[quarter],
            send_sem=parts_sem.at[0],
            recv_sem=parts_sem.at[1],
            device_id=quarter_peer(step),
            device_id_type=MESH,
        ).start()
        return carry

    lax.fori_loop(1, quarters, send_part, 0)

    def pair_at(step):
        return step

    def tail_copy(step):
        pair = pair_at(step)
        return pltpu.make_async_remote_copy(
            src_ref=tail_out.at[pair],
            dst_ref=tail_in.at[pair],
            send_sem=tail_send.at[step],
            recv_sem=tail_recv.at[step],
            device_id=partner,
            device_id_type=MESH,
        )

    def send_tail(step, carry):
        tail_copy(step).start()
        return carry

    lax.fori_loop(0, pairs, send_tail, 0)

    def wait_all(buffer, count, sem):
        span = buffer.at[pl.ds(0, count)]
        pltpu.make_async_copy(span, span, sem).wait()

    loads[5].wait()
    normalize_all(k_buf, k_hat, k_inv)

    wait_all(parts, quarters - 1, parts_sem.at[1])
    gains[head] = jnp.sum(parts[...], axis=0)

    def send_gain(peer):
        pltpu.make_async_remote_copy(
            src_ref=gains.at[head],
            dst_ref=gains.at[head],
            send_sem=gains_send.at[0],
            recv_sem=gains_recv.at[head],
            device_id=peer,
            device_id_type=MESH,
        ).start()

    by_line(send_gain, lambda step: pairs - 1 - step)

    loads[6].wait()
    sender = jnp.broadcast_to(sends_ref[0, 0], (tail, 2 * DH)) == 1
    low = keep // 16 * 16
    fixed = keep - low

    def attend(pair):
        indices = (pair, pair + pairs)
        lanes = [lanes_of(i) for i in indices]
        gain_q = [gains[i, 0:1, :] for i in indices]
        gain_k = [gains[i, 1:2, :] for i in indices]
        moved = tail_in[pair].astype(jnp.float32)
        moved = side_by_side([moved[:tail], moved[tail:]])
        edge = side_by_side([g_buf[low:rows, at] for at in lanes]).astype(jnp.float32)
        edge = jnp.concatenate([edge[:fixed], jnp.where(sender, moved, edge[fixed:])], axis=0)
        grads = side_by_side([g_buf[:low, at] for at in lanes])
        grads = jnp.concatenate([grads, edge.astype(jnp.bfloat16)], axis=0)
        query_hat = [q_hat[:, at] for at in lanes]
        key_hat = [k_hat[:, at] for at in lanes]
        query_norm = [(hat * gain).astype(jnp.bfloat16) for hat, gain in zip(query_hat, gain_q)]
        key_norm = [(hat * gain).astype(jnp.bfloat16) for hat, gain in zip(key_hat, gain_k)]
        keys = diagonal(*key_norm)
        scores = dot(side_by_side(query_norm), keys, 1)
        grad_probs = dot(grads, diagonal(*[v_buf[:, at] for at in lanes]), 1)
        grad_scores = []
        for i in range(2):
            half = slice(i * rows, (i + 1) * rows)
            weights = jnp.exp2(scores[:, half] * EXP_SCALE) * same[...]
            probs = grad_probs[:, half]
            scale = 1.0 / jnp.sum(weights, axis=-1, keepdims=True)
            carried = jnp.sum(weights * probs, axis=-1, keepdims=True) * scale
            grad_scores.append((weights * (scale * SCALE) * (probs - carried)).astype(jnp.bfloat16))
        grad_qn = dot(side_by_side(grad_scores), keys, 0)
        grad_kn = dot(side_by_side([x.T for x in grad_scores]), diagonal(*query_norm), 0)
        for i, index in enumerate(indices):
            half = slice(i * DH, (i + 1) * DH)
            at = lanes[i]
            grad_q, term_q = norm_backward(grad_qn[:, half], query_hat[i], q_inv[:, at], gain_q[i])
            grad_k, term_k = norm_backward(grad_kn[:, half], key_hat[i], k_inv[:, at], gain_k[i])
            dq_buf[:, at] = grad_q
            dk_buf[:, at] = grad_k
            terms[index, 0:1, :] = term_q
            terms[index, 1:2, :] = term_k

    def attend_batch(start, count):
        todo = [pair_at(start + i) for i in range(count)]
        for i, pair in enumerate(todo):
            for index in (pair, pair + pairs):

                @pl.when(index != head)
                def _():
                    row = gains.at[index]
                    pltpu.make_async_copy(row, row, gains_recv.at[index]).wait()

            tail_copy(start + i).wait()
        for pair in todo:
            attend(pair)
        for pair in todo:
            for index in (pair, pair + pairs):

                @pl.when(index != head)
                def _():
                    pltpu.make_async_remote_copy(
                        src_ref=terms.at[index],
                        dst_ref=first.at[head],
                        send_sem=first_sem.at[0],
                        recv_sem=first_sem.at[1],
                        device_id=(index * quarters + quarter, g),
                        device_id_type=MESH,
                    ).start()

        for pair in todo:
            for index in (pair, pair + pairs):
                at = lanes_of(index)
                pltpu.make_async_copy(dq_buf.at[:, at], dq_out.at[:, at], store_sem.at[0]).start()
                pltpu.make_async_copy(dk_buf.at[:, at], dk_out.at[:, at], store_sem.at[1]).start()

    def attend_two(turn, carry):
        attend_batch(1 + turn * 2, 2)
        return carry

    attend_batch(0, 1)
    lax.fori_loop(0, (pairs - 1) // 2, attend_two, 0)
    if pairs % 2 == 0:
        attend_batch(pairs - 1, 1)

    first[head] = terms[head]
    wait_all(first, heads - 1, first_sem.at[1])
    last[mine] = jnp.sum(first[...], axis=0)

    for peer in crew_peers:
        pltpu.make_async_remote_copy(
            src_ref=last.at[mine],
            dst_ref=last.at[mine],
            send_sem=last_sem.at[0],
            recv_sem=last_sem.at[1],
            device_id=peer,
            device_id_type=MESH,
        ).start()
    wait_all(parts, quarters - 1, parts_sem.at[0])
    wait_all(gains, heads - 1, gains_send.at[0])
    wait_all(first, heads - 1, first_sem.at[0])
    pltpu.make_async_copy(dq_buf, dq_out, store_sem.at[0]).wait()
    pltpu.make_async_copy(dk_buf, dk_out, store_sem.at[1]).wait()
    wait_all(last, crew - 1, last_sem.at[0])
    wait_all(last, crew - 1, last_sem.at[1])
    total = jnp.sum(last[...], axis=0)
    piece = jnp.zeros((2, width), jnp.float32)
    for i in range(quarters):
        piece += jnp.where(quarter == i, total[:, i * width : (i + 1) * width], 0.0)
    for i in range(2):
        gains_out[i] = piece[i : i + 1]


def finish(dq_in, dk_in, gains_in, dq_out, dk_out, gain_q_out, gain_k_out, sem):
    rows = dq_in.shape[0]
    chunk = rows // CHUNKS
    copies = [
        pltpu.make_async_copy(
            src.at[pl.ds(i * chunk, chunk)], dst.at[pl.ds(i * chunk, chunk)], sem.at[j * CHUNKS + i]
        )
        for i in range(CHUNKS)
        for j, (src, dst) in enumerate(((dq_in, dq_out), (dk_in, dk_out)))
    ]
    copies += [
        pltpu.make_async_copy(gains_in.at[i], out, sem.at[2 * CHUNKS + i])
        for i, out in enumerate((gain_q_out, gain_k_out))
    ]
    for copy in copies:
        copy.start()
    for copy in copies:
        copy.wait()


def body(query_rows, key_rows, value_rows, out_grad, query_gain, key_gain, image_sizes, sends_tail):
    _, _, rows, wid = query_rows.shape
    grad_rows = out_grad.shape[2]
    tail = grad_rows - rows
    heads = wid // DH
    quarters = lax.axis_size("fsdp") // heads
    groups = lax.axis_size("group")
    pairs = heads // 2
    crew = quarters * groups
    width = DH // quarters
    any_spec = pl.BlockSpec(memory_space=pl.ANY)
    vmem = pl.BlockSpec(memory_space=pltpu.VMEM)
    wide = (rows, wid)
    dma = pltpu.SemaphoreType.DMA
    images = image_sizes.shape[-1]
    operands = (
        query_rows.reshape(wide),
        key_rows.reshape(wide),
        value_rows.reshape(wide),
        out_grad.reshape(grad_rows, wid),
        query_gain.reshape(1, width),
        key_gain.reshape(1, width),
        image_sizes.reshape(1, images),
    )
    dq, dk, gains = pl.pallas_call(
        functools.partial(kernel, (heads, quarters, groups, rows, tail)),
        out_shape=(
            jax.ShapeDtypeStruct(wide, jnp.bfloat16),
            jax.ShapeDtypeStruct(wide, jnp.bfloat16),
            jax.ShapeDtypeStruct((2, 1, width), jnp.float32),
        ),
        in_specs=[any_spec] * 7 + [pl.BlockSpec(memory_space=pltpu.SMEM)],
        out_specs=(any_spec, any_spec, vmem),
        scratch_shapes=[
            pltpu.VMEM(wide, jnp.bfloat16),
            pltpu.VMEM(wide, jnp.bfloat16),
            pltpu.VMEM(wide, jnp.bfloat16),
            pltpu.VMEM((grad_rows, wid), jnp.bfloat16),
            pltpu.VMEM((2, 1, width), jnp.float32),
            pltpu.SMEM((1, images), jnp.int32),
            pltpu.VMEM(wide, jnp.float32),
            pltpu.VMEM(wide, jnp.float32),
            pltpu.VMEM(wide, jnp.float32),
            pltpu.VMEM(wide, jnp.float32),
            pltpu.VMEM(wide, jnp.bfloat16),
            pltpu.VMEM(wide, jnp.bfloat16),
            pltpu.VMEM((rows, rows), jnp.float32),
            pltpu.VMEM((pairs, 2 * tail, DH), jnp.bfloat16),
            pltpu.VMEM((pairs, 2 * tail, DH), jnp.bfloat16),
            pltpu.VMEM((quarters, 2, DH), jnp.float32),
            pltpu.VMEM((heads, 2, DH), jnp.float32),
            pltpu.VMEM((heads, 2, DH), jnp.float32),
            pltpu.VMEM((heads, 2, DH), jnp.float32),
            pltpu.VMEM((crew, 2, DH), jnp.float32),
            dma((7,)),
            dma((2,)),
            dma((2,)),
            dma((1,)),
            dma((heads,)),
            dma((pairs,)),
            dma((pairs,)),
            dma((2,)),
            dma((2,)),
        ],
        compiler_params=pltpu.CompilerParams(
            collective_id=0, has_side_effects=True, vmem_limit_bytes=VMEM_LIMIT
        ),
    )(*[pltpu.with_memory_space_constraint(x, pltpu.HBM) for x in operands], sends_tail)
    dq, dk, gain_q, gain_k = pl.pallas_call(
        finish,
        out_shape=(
            jax.ShapeDtypeStruct(wide, jnp.bfloat16),
            jax.ShapeDtypeStruct(wide, jnp.bfloat16),
            jax.ShapeDtypeStruct((1, width), jnp.float32),
            jax.ShapeDtypeStruct((1, width), jnp.float32),
        ),
        in_specs=[vmem, vmem, vmem],
        out_specs=(any_spec,) * 4,
        scratch_shapes=[dma((2 * CHUNKS + 2,))],
    )(*[pltpu.with_memory_space_constraint(x, pltpu.VMEM) for x in (dq, dk, gains)])
    return dq[None, None], dk[None, None], gain_q.reshape(width), gain_k.reshape(width)


def solution(mesh):
    placed = (
        P("fsdp", "group", None, None),
        P("fsdp", "group", None, None),
        P("fsdp", "group", None, None),
        P("fsdp", "group", None, None),
        P("fsdp"),
        P("fsdp"),
        P("fsdp", "group", None),
        P("fsdp", "group"),
    )
    return jax.shard_map(
        body,
        mesh=mesh,
        in_specs=placed,
        out_specs=(
            P("fsdp", "group", None, None),
            P("fsdp", "group", None, None),
            P("fsdp"),
            P("fsdp"),
        ),
        check_vma=False,
    )
```
